32 devices in a mesh: slab: 2 (over x), blk: 16 (over z, y, core).
Axes of the slice: x: 2, y: 2, z: 4, core: 2. Of those that a mesh axis runs over, the one named last changes fastest.
Arguments:
- expression: bfloat16 [768, 4096], P('blk', 'slab'), parts along dimension 1, may hold values from -400 to 400
- dosages: bfloat16 [768, 32768], P(None, ('slab', 'blk')), parts along dimension 1, may hold values from -400 to 400
- covariates: float32 [64, 768], replicated, may hold values from -6 to 6
- window_blocks: int32 [32, 16], P(('slab', 'blk')), parts along dimension 0, may hold values from 0 to 127, as said below
- window_counts: int32 [32], P(('slab', 'blk')), parts along dimension 0, may hold values from 10 to 16
Outputs:
- scores: float32 [32, 16, 128, 128], P(('slab', 'blk')), parts along dimension 0
The draws below stay inside these ranges and needn't reach their ends.
There are 2 independent parts, one for each index of `slab`. The reference program is written for one: setup_inputs(seed, part) draws one part's arguments, and reference() takes and returns one part's arrays. A program takes and returns all parts, laid end to end along the dimension named above; an argument that names none is the same for every part. Nothing has to cross between parts.
Inputs may be any that keep to these rules, and one draw needn't show every extreme that they name: `window_blocks`: row b lists window_counts[b] consecutive variant blocks followed by repeats of its first, all among the variant blocks of the device that owns gene block b (block b) and of its two neighbours.
All inputs are finite; a program needn't handle non-finite values.
Results may differ from the reference program's by a relative error of at most 0.0039.
Values may be sent and summed in bfloat16 or wider, within the bound.
A program may use at most 128 MiB of HBM per device.

```python
import math
import jax
import jax.numpy as jnp
from jax import lax

K = 64
BS = 128
GB_DEV = 1
VB_DEV = 8
MOST = 16
SAMPLES = 768
GBLOCKS = 16
VBLOCKS = 128
GENES = 2048
VARIANTS = 16384


def window_plan(key):
    count_key, force_key, start_key = jax.random.split(key, 3)
    counts = jax.random.randint(count_key, (GBLOCKS,), MOST // 2 + 2, MOST + 1)
    forced = jax.random.randint(force_key, (), 0, GBLOCKS)
    counts = jnp.where(jnp.arange(GBLOCKS) == forced, MOST, counts)
    owner = jnp.arange(GBLOCKS) // GB_DEV
    within = jnp.arange(GBLOCKS) % GB_DEV
    lowest = jnp.maximum(0, (owner - 1) * VB_DEV)
    highest = jnp.minimum(VBLOCKS, (owner + 2) * VB_DEV)
    latest = highest - counts
    high_bound = jnp.where(within == 0, jnp.minimum(latest, owner * VB_DEV - 1), latest)
    high_bound = jnp.maximum(high_bound, lowest)
    low_bound = jnp.where(within == GB_DEV - 1, jnp.maximum(lowest, (owner + 1) * VB_DEV + 1 - counts), lowest)
    low_bound = jnp.minimum(low_bound, high_bound)
    first_block = jax.random.randint(start_key, (GBLOCKS,), low_bound, high_bound + 1)
    slot_index = jnp.arange(MOST)[None, :]
    blocks = first_block[:, None] + jnp.where(slot_index < counts[:, None], slot_index, 0)
    return (blocks.astype(jnp.int32), counts.astype(jnp.int32))


def draw_window_blocks(key, part):
    return window_plan(key)[0]


def draw_window_counts(key, part):
    return window_plan(key)[1]


def scaled_field(key, row_total, column_total, top):
    normal_key = jax.random.fold_in(key, 0)
    row_key = jax.random.fold_in(key, 2)
    column_key = jax.random.fold_in(key, 3)
    gaussian = jnp.clip(jax.random.normal(normal_key, (row_total, column_total), jnp.float32), -4.0, 4.0)
    base = gaussian
    row_scale = jnp.exp(jax.random.uniform(row_key, (row_total, 1), jnp.float32, 0.0, jnp.log(top)))
    column_scale = jnp.exp(jax.random.uniform(column_key, (1, column_total), jnp.float32, 0.0, jnp.log(top)))
    return base * row_scale * column_scale


def draw_dosages(key, part):
    key = jax.random.fold_in(key, 11)
    return scaled_field(key, SAMPLES, VARIANTS, 10.0).astype(jnp.bfloat16)


def draw_expression(key, part):
    key = jax.random.fold_in(key, 12)
    return scaled_field(key, SAMPLES, GENES, 10.0).astype(jnp.bfloat16)


def centred(rng, extent, deviation, most, held_as=jnp.bfloat16):
    result = deviation * jax.random.normal(rng, extent, jnp.float32)
    return jnp.clip(result, min=-most, max=most).astype(held_as)


def setup_inputs(seed: int = 0, part: int = 0) -> dict:
    streams_of = jax.random.split(jax.random.key(seed), 6)
    part_splits = jax.random.split(jax.random.fold_in(streams_of[5], part), 6)
    expression = draw_expression(jax.random.fold_in(jax.random.fold_in(streams_of[5], part), 71), part)
    dosages = draw_dosages(jax.random.fold_in(jax.random.fold_in(streams_of[5], part), 71), part)
    covariates = centred(streams_of[2], (K, SAMPLES), 1.0, 6.0, jnp.float32)
    window_blocks = draw_window_blocks(jax.random.fold_in(jax.random.fold_in(streams_of[5], part), 71), part)
    window_counts = draw_window_counts(jax.random.fold_in(jax.random.fold_in(streams_of[5], part), 71), part)
    return dict(expression=expression, dosages=dosages, covariates=covariates, window_blocks=window_blocks, window_counts=window_counts)


def residualize(values, covariates, factor):
    projected = jnp.dot(covariates, values, precision=lax.Precision.HIGHEST)
    middle = lax.linalg.triangular_solve(factor, projected, left_side=True, lower=True, transpose_a=False)
    coefficients = lax.linalg.triangular_solve(factor, middle, left_side=True, lower=True, transpose_a=True)
    residuals = values - jnp.dot(covariates.T, coefficients, precision=lax.Precision.HIGHEST)
    column_scale = lax.rsqrt(lax.optimization_barrier(jnp.mean(residuals * residuals, axis=0)) + 1e-06)
    return (residuals * column_scale).astype(jnp.bfloat16)

def reference(expression, dosages, covariates, window_blocks, window_counts):
    factor = jnp.linalg.cholesky(jnp.dot(covariates, covariates.T, precision=lax.Precision.HIGHEST))
    gene_tiles = expression.reshape(SAMPLES, GBLOCKS, BS).transpose(1, 0, 2)
    gene_ready = lax.map(lambda tile: residualize(tile.astype(jnp.float32), covariates, factor), gene_tiles)
    panel_tiles = dosages.reshape(SAMPLES, VBLOCKS, BS).transpose(1, 0, 2)
    panel_ready = lax.map(lambda tile: residualize(tile.astype(jnp.float32), covariates, factor), panel_tiles)
    factor_z = math.sqrt(SAMPLES - K) / SAMPLES
    slot_index = jnp.arange(MOST)

    def one_block(inputs):
        window_ids, count, gene_tile = inputs
        chosen = panel_ready[window_ids].astype(jnp.float32)
        product = jnp.einsum('mnv,ng->mvg', chosen, gene_tile.astype(jnp.float32))
        return jnp.where((slot_index < count)[:, None, None], product * factor_z, 0.0)
    return lax.map(one_block, (window_blocks, window_counts, gene_ready))
```

```python
import functools
import math

import jax
import jax.numpy as jnp
from jax import lax
from jax.experimental import pallas as pl
from jax.experimental.pallas import tpu as pltpu
from jax.sharding import PartitionSpec as P

BS = 128
PANEL = 4
MESH = pl.DeviceIdType.MESH
F32 = jnp.float32
BF16 = jnp.bfloat16
NT = (((1,), (1,)), ((), ()))


def split3(x):
    high = x.astype(BF16)
    rest = x - high.astype(F32)
    middle = rest.astype(BF16)
    low = (rest - middle.astype(F32)).astype(BF16)
    return high, middle, low


def whitened(cov):
    k = cov.shape[0]
    zeros = jnp.zeros_like(cov)
    gram = lax.dot_general(
        cov,
        jnp.concatenate([cov, zeros], axis=0),
        NT,
        precision=lax.Precision.HIGHEST,
        preferred_element_type=F32,
    )
    lane = lax.broadcasted_iota(jnp.int32, (8, 2 * k), 1)
    sub = lax.broadcasted_iota(jnp.int32, (8, 2 * k), 0)
    tiles = []
    for t in range(k // 8):
        unit = (lane - k == sub + 8 * t).astype(F32)
        tiles.append(jnp.where(lane < k, gram[8 * t : 8 * t + 8, :], unit))
    for first in range(0, k, PANEL):
        home = first // 8
        live = range(home, k // 8)
        columns = [
            {t: jnp.broadcast_to(tiles[t][:, first + j : first + j + 1], (8, 2 * k)) for t in live}
            for j in range(PANEL)
        ]
        rows = [tiles[home][first % 8 + j : first % 8 + j + 1, :] for j in range(PANEL)]
        for j in range(PANEL):
            at = first % 8 + j
            inverse = 1.0 / columns[j][home][at : at + 1, :]
            factors = {t: columns[j][t] * inverse for t in live}
            factors[home] = jnp.where(sub > at, factors[home], 0.0)
            for later in range(j + 1, PANEL):
                cross = columns[later][home][at : at + 1, :]
                for t in live:
                    columns[later][t] = columns[later][t] - factors[t] * cross
                where = first % 8 + later
                rows[later] = rows[later] - factors[home][where : where + 1, :] * rows[j]
            for t in live:
                tiles[t] = tiles[t] - factors[t] * rows[j]
    scaled = []
    for t in range(k // 8):
        diagonal = jnp.sum(jnp.where(lane == sub + 8 * t, tiles[t], 0.0), axis=1, keepdims=True)
        scaled.append(jnp.where(lane < k, 0.0, tiles[t]) * lax.rsqrt(diagonal))
    inverse_factor = jnp.concatenate(scaled, axis=0)
    return jnp.dot(
        inverse_factor,
        jnp.concatenate([zeros, cov], axis=0),
        precision=lax.Precision.HIGHEST,
        preferred_element_type=F32,
    )


def kernel(
    n, scale,
    expr_ref, dos_ref, cov_ref,
    out_ref,
    cov_v, dos_v, vt, graw, g_own, g_left, g_right, p_own, p_left, p_right, q6, qd, qt6,
    local_sem, a2a_send, a2a_recv, g_send, g_recv, p_send, p_recv,
):
    me = lax.axis_index("blk")
    samples, width = dos_v.shape
    part = expr_ref.shape[0]
    panels = width // BS
    k = cov_v.shape[0]

    cov_copy = pltpu.make_async_copy(cov_ref, cov_v, local_sem.at[0])
    cov_copy.start()
    dos_copy = pltpu.make_async_copy(dos_ref, dos_v, local_sem.at[1])
    dos_copy.start()

    def columns_of(j):
        return expr_ref.at[:, pl.ds(pl.multiple_of(j * BS, BS), BS)]

    mine = graw.at[pl.ds(pl.multiple_of(me * part, 16), part), :]
    own_copy = pltpu.make_async_copy(columns_of(me), mine, local_sem.at[2])
    own_copy.start()

    barrier = pltpu.get_barrier_semaphore()

    @pl.loop(1, n)
    def _(s):
        pl.semaphore_signal(
            barrier, inc=1, device_id={"blk": lax.rem(me + s, n)}, device_id_type=MESH
        )

    pl.semaphore_wait(barrier, n - 1)

    def exchange(s):
        peer = lax.rem(me + s, n)
        return pltpu.make_async_remote_copy(
            src_ref=columns_of(peer),
            dst_ref=mine,
            send_sem=a2a_send.at[s],
            recv_sem=a2a_recv.at[s],
            device_id={"blk": peer},
            device_id_type=MESH,
        )

    @pl.loop(1, n)
    def _(s):
        exchange(s).start()

    cov_copy.wait()
    dos_copy.wait()

    @pl.loop(0, panels)
    def _(c):
        at = pl.multiple_of(c * BS, BS)
        vt[pl.ds(at, BS), :] = dos_v[:, pl.ds(at, BS)].T

    q = whitened(cov_v[...])
    qh, qm, ql = split3(q)
    q6[...] = jnp.concatenate([qh, qm, qh, qm, qh, ql], axis=0)
    qd[...] = jnp.concatenate([qh, qh, qm, qm, ql, ql], axis=0)
    first = q6[0 : 2 * k, :].T
    qt6[:, 0 : 2 * k] = first
    qt6[:, 2 * k : 4 * k] = first
    qt6[:, 4 * k : 6 * k] = q6[4 * k : 6 * k, :].T

    @pl.loop(0, panels)
    def _(c):
        at = pl.multiple_of(c * BS, BS)
        v = vt[pl.ds(at, BS), :]
        w3 = lax.dot_general(v, qd[...], NT, preferred_element_type=F32)
        w = w3[:, 0 : 2 * k] + w3[:, 2 * k : 4 * k] + w3[:, 4 * k : 6 * k]
        wh, wm, wl = split3(w)
        lane = lax.broadcasted_iota(jnp.int32, w.shape, 1)
        last = jnp.where(lane < k, wl.astype(F32), wh.astype(F32)).astype(BF16)
        w6 = jnp.concatenate([wh, wm, last], axis=1)
        res = v.astype(F32) - jnp.dot(w6, q6[...], preferred_element_type=F32)
        mean = jnp.sum(res * res, axis=1, keepdims=True) * (1.0 / samples)
        vt[pl.ds(at, BS), :] = (res * lax.rsqrt(mean + 1e-06)).astype(BF16)

    own_copy.wait()

    @pl.loop(1, n)
    def _(s):
        exchange(s).wait_recv()

    g = graw[...]
    w3 = jnp.dot(
        jnp.concatenate([q6[0 : 2 * k, :], q6[5 * k : 6 * k, :]], axis=0),
        g,
        preferred_element_type=F32,
    )
    wh, wm, wl = split3(w3[0:k, :] + w3[k : 2 * k, :] + w3[2 * k : 3 * k, :])
    w6 = jnp.concatenate([wh, wh, wm, wm, wl, wh], axis=0)
    res = g.astype(F32) - jnp.dot(qt6[...], w6, preferred_element_type=F32)
    mean = jnp.sum(res * res, axis=0, keepdims=True) * (1.0 / samples)
    g_own[...] = (res * lax.rsqrt(mean + 1e-06)).astype(BF16)

    def send(src, dst, sems, slot, peer):
        return pltpu.make_async_remote_copy(
            src_ref=src,
            dst_ref=dst,
            send_sem=sems[0].at[slot],
            recv_sem=sems[1].at[slot],
            device_id={"blk": peer},
            device_id_type=MESH,
        )

    genes_left = send(g_own, g_right, (g_send, g_recv), 0, me - 1)
    genes_right = send(g_own, g_left, (g_send, g_recv), 1, me + 1)
    back_left = send(
        p_left, out_ref.at[pl.ds(2 * width, width), :], (p_send, p_recv), 0, me - 1
    )
    back_right = send(p_right, out_ref.at[pl.ds(0, width), :], (p_send, p_recv), 1, me + 1)
    has_left = me > 0
    has_right = me < n - 1

    @pl.when(has_left)
    def _():
        genes_left.start()

    @pl.when(has_right)
    def _():
        genes_right.start()

    def multiply(genes, target):
        @pl.loop(0, panels // 2)
        def _(c):
            at = pl.multiple_of(c * 2 * BS, 2 * BS)
            product = jnp.dot(
                vt[pl.ds(at, 2 * BS), :], genes[...], preferred_element_type=F32
            )
            target[pl.ds(at, 2 * BS), :] = (product * scale).astype(BF16)

    multiply(g_own, p_own)
    keep = pltpu.make_async_copy(p_own, out_ref.at[pl.ds(width, width), :], local_sem.at[3])
    keep.start()

    @pl.when(has_left)
    def _():
        genes_right.wait_recv()
        multiply(g_left, p_left)
        back_left.start()

    @pl.when(has_right)
    def _():
        genes_left.wait_recv()
        multiply(g_right, p_right)
        back_right.start()

    keep.wait()

    @pl.loop(1, n)
    def _(s):
        exchange(s).wait_send()

    @pl.when(has_left)
    def _():
        genes_left.wait_send()
        back_left.wait_send()
        back_right.wait_recv()

    @pl.when(has_right)
    def _():
        genes_right.wait_send()
        back_right.wait_send()
        back_left.wait_recv()


def on_device(expression, dosages, covariates, window_blocks, window_counts):
    n = lax.axis_size("blk")
    samples, width = dosages.shape
    panels = width // BS
    k = covariates.shape[0]
    slots = window_blocks.shape[1]
    scale = math.sqrt(samples - k) / samples
    any_space = pl.BlockSpec(memory_space=pl.ANY)
    blocks = 3 * panels + slots
    products = pl.pallas_call(
        functools.partial(kernel, n, scale),
        out_shape=jax.ShapeDtypeStruct((blocks * BS, BS), BF16),
        in_specs=[any_space] * 3,
        out_specs=any_space,
        scratch_shapes=[
            pltpu.VMEM((k, samples), F32),
            pltpu.VMEM((samples, width), BF16),
            pltpu.VMEM((width, samples), BF16),
            pltpu.VMEM((samples, BS), BF16),
            pltpu.VMEM((samples, BS), BF16),
            pltpu.VMEM((samples, BS), BF16),
            pltpu.VMEM((samples, BS), BF16),
            pltpu.VMEM((width, BS), BF16),
            pltpu.VMEM((width, BS), BF16),
            pltpu.VMEM((width, BS), BF16),
            pltpu.VMEM((6 * k, samples), BF16),
            pltpu.VMEM((6 * k, samples), BF16),
            pltpu.VMEM((samples, 6 * k), BF16),
            pltpu.SemaphoreType.DMA((4,)),
            pltpu.SemaphoreType.DMA((n,)),
            pltpu.SemaphoreType.DMA((n,)),
            pltpu.SemaphoreType.DMA((2,)),
            pltpu.SemaphoreType.DMA((2,)),
            pltpu.SemaphoreType.DMA((2,)),
            pltpu.SemaphoreType.DMA((2,)),
        ],
        compiler_params=pltpu.CompilerParams(
            collective_id=0, has_side_effects=True, vmem_limit_bytes=50 * 1024 * 1024
        ),
    )(expression, dosages, covariates)
    first = window_blocks[0, 0] - (lax.axis_index("blk") - 1) * panels
    listed = lax.dynamic_slice_in_dim(products.reshape(blocks, BS, BS), first, slots, axis=0)
    live = jnp.arange(slots)[None, :] < window_counts[:, None]
    return jnp.where(live[:, :, None, None], listed[None].astype(F32), 0.0)


def solution(mesh):
    in_specs = (
        P("blk", "slab"),
        P(None, ("slab", "blk")),
        P(),
        P(("slab", "blk"), None),
        P(("slab", "blk")),
    )
    out_specs = P(("slab", "blk"), None, None, None)
    return jax.shard_map(
        on_device, mesh=mesh, in_specs=in_specs, out_specs=out_specs, check_vma=False
    )
```

```python
import functools
import math

import jax
import jax.numpy as jnp
from jax import lax
from jax.experimental import pallas as pl
from jax.experimental.pallas import tpu as pltpu
from jax.sharding import PartitionSpec as P

BS = 128
PANEL = 4
ROWS = 256
VMEM_BYTES = 63 * 10**6
MESH = pl.DeviceIdType.MESH
F32 = jnp.float32
BF16 = jnp.bfloat16
NT = (((1,), (1,)), ((), ()))


def split3(x):
    high = x.astype(BF16)
    rest = x - high.astype(F32)
    middle = rest.astype(BF16)
    low = (rest - middle.astype(F32)).astype(BF16)
    return high, middle, low


def whitened(cov):
    k = cov.shape[0]
    zeros = jnp.zeros_like(cov)
    gram = lax.dot_general(
        cov,
        jnp.concatenate([cov, zeros], axis=0),
        NT,
        precision=lax.Precision.HIGHEST,
        preferred_element_type=F32,
    )
    lane = lax.broadcasted_iota(jnp.int32, (8, 2 * k), 1)
    sub = lax.broadcasted_iota(jnp.int32, (8, 2 * k), 0)
    tiles = []
    for t in range(k // 8):
        unit = (lane - k == sub + 8 * t).astype(F32)
        tiles.append(jnp.where(lane < k, gram[8 * t : 8 * t + 8, :], unit))
    for first in range(0, k, PANEL):
        home = first // 8
        live = range(home, k // 8)
        columns = [
            {t: jnp.broadcast_to(tiles[t][:, first + j : first + j + 1], (8, 2 * k)) for t in live}
            for j in range(PANEL)
        ]
        rows = [tiles[home][first % 8 + j : first % 8 + j + 1, :] for j in range(PANEL)]
        for j in range(PANEL):
            at = first % 8 + j
            inverse = 1.0 / columns[j][home][at : at + 1, :]
            factors = {t: columns[j][t] * inverse for t in live}
            factors[home] = jnp.where(sub > at, factors[home], 0.0)
            for later in range(j + 1, PANEL):
                cross = columns[later][home][at : at + 1, :]
                for t in live:
                    columns[later][t] = columns[later][t] - factors[t] * cross
                where = first % 8 + later
                rows[later] = rows[later] - factors[home][where : where + 1, :] * rows[j]
            for t in live:
                tiles[t] = tiles[t] - factors[t] * rows[j]
    scaled = []
    for t in range(k // 8):
        diagonal = jnp.sum(jnp.where(lane == sub + 8 * t, tiles[t], 0.0), axis=1, keepdims=True)
        scaled.append(jnp.where(lane < k, 0.0, tiles[t]) * lax.rsqrt(diagonal))
    inverse_factor = jnp.concatenate(scaled, axis=0)
    return jnp.dot(
        inverse_factor,
        jnp.concatenate([zeros, cov], axis=0),
        precision=lax.Precision.HIGHEST,
        preferred_element_type=F32,
    )


def kernel(
    n, scale, rows,
    expr_ref, dos_ref, cov_ref,
    out_ref,
    cov_v, dos_v, vt, graw, p_own, p_left, p_right, q6, qd, qt6,
    local_sem, a2a_send, a2a_recv, g_send, g_recv, p_send, p_recv,
):
    me = lax.axis_index("blk")
    samples, width = dos_v.shape
    part = expr_ref.shape[0]
    k = cov_v.shape[0]
    has_left = me > 0
    has_right = me < n - 1

    def columns_of(j):
        return expr_ref.at[:, pl.ds(pl.multiple_of(j * BS, BS), BS)]

    barrier = pltpu.get_barrier_semaphore()

    @pl.loop(1, n)
    def _(s):
        pl.semaphore_signal(
            barrier, inc=1, device_id={"blk": lax.rem(me + s, n)}, device_id_type=MESH
        )

    cov_copy = pltpu.make_async_copy(cov_ref, cov_v, local_sem.at[0])
    cov_copy.start()
    dos_copy = pltpu.make_async_copy(dos_ref, dos_v, local_sem.at[1])
    dos_copy.start()
    mine = graw.at[1, pl.ds(pl.multiple_of(me * part, 16), part), :]
    own_copy = pltpu.make_async_copy(columns_of(me), mine, local_sem.at[2])
    own_copy.start()

    def remote(src, dst, sems, slot, peer):
        return pltpu.make_async_remote_copy(
            src_ref=src,
            dst_ref=dst,
            send_sem=sems[0].at[slot],
            recv_sem=sems[1].at[slot],
            device_id={"blk": peer},
            device_id_type=MESH,
        )

    def exchange(s):
        peer = lax.rem(me + s, n)
        return remote(columns_of(peer), mine, (a2a_send, a2a_recv), s, peer)

    pl.semaphore_wait(barrier, n - 1)

    @pl.loop(1, n)
    def _(s):
        exchange(s).start()

    cov_copy.wait()
    q = whitened(cov_v[...])
    qh, qm, ql = split3(q)
    q6[...] = jnp.concatenate([qh, qm, qh, qm, qh, ql], axis=0)
    qd[...] = jnp.concatenate([qh, qh, qm, qm, ql, ql], axis=0)
    first = q6[0 : 2 * k, :].T
    qt6[:, 0 : 2 * k] = first
    qt6[:, 2 * k : 4 * k] = first
    qt6[:, 4 * k : 6 * k] = q6[4 * k : 6 * k, :].T

    dos_copy.wait()

    def variants(at):
        v = dos_v[:, pl.ds(at, rows)].T
        w3 = lax.dot_general(v, qd[...], NT, preferred_element_type=F32)
        w = w3[:, 0 : 2 * k] + w3[:, 2 * k : 4 * k] + w3[:, 4 * k : 6 * k]
        wh, wm, wl = split3(w)
        lane = lax.broadcasted_iota(jnp.int32, w.shape, 1)
        last = jnp.where(lane < k, wl.astype(F32), wh.astype(F32)).astype(BF16)
        w6 = jnp.concatenate([wh, wm, last], axis=1)
        res = v.astype(F32) - jnp.dot(w6, q6[...], preferred_element_type=F32)
        mean = jnp.sum(res * res, axis=1, keepdims=True) * (1.0 / samples)
        vt[pl.ds(at, rows), :] = (res * lax.rsqrt(mean + 1e-06)).astype(BF16)

    half = width // 2

    @pl.loop(0, half // rows)
    def _(c):
        variants(pl.multiple_of(c * rows, rows))

    own_copy.wait()

    @pl.loop(1, n)
    def _(s):
        exchange(s).wait_recv()

    genes_left = remote(graw.at[1], graw.at[2], (g_send, g_recv), 0, me - 1)
    genes_right = remote(graw.at[1], graw.at[0], (g_send, g_recv), 1, me + 1)

    @pl.when(has_left)
    def _():
        genes_left.start()

    @pl.when(has_right)
    def _():
        genes_right.start()

    @pl.loop(half // rows, width // rows)
    def _(c):
        variants(pl.multiple_of(c * rows, rows))

    def genes(raw):
        w3 = jnp.dot(
            jnp.concatenate([q6[0 : 2 * k, :], q6[5 * k : 6 * k, :]], axis=0),
            raw,
            preferred_element_type=F32,
        )
        wh, wm, wl = split3(w3[0:k, :] + w3[k : 2 * k, :] + w3[2 * k : 3 * k, :])
        w6 = jnp.concatenate([wh, wh, wm, wm, wl, wh], axis=0)
        res = raw.astype(F32) - jnp.dot(qt6[...], w6, preferred_element_type=F32)
        mean = jnp.sum(res * res, axis=0, keepdims=True) * (1.0 / samples)
        return (res * lax.rsqrt(mean + 1e-06)).astype(BF16)

    pieces = 4
    step = width // pieces

    own = genes(graw[1])
    for c in range(pieces):
        product = jnp.dot(vt[c * step : (c + 1) * step, :], own, preferred_element_type=F32)
        p_own[c * step : (c + 1) * step, :] = (product * scale).astype(BF16)
    keep = pltpu.make_async_copy(p_own, out_ref.at[pl.ds(width, width), :], local_sem.at[3])
    keep.start()

    @pl.when(has_left)
    def _():
        genes_right.wait_recv()

    @pl.when(has_right)
    def _():
        genes_left.wait_recv()

    @pl.when(jnp.logical_not(has_left))
    def _():
        graw[0] = graw[1]

    @pl.when(jnp.logical_not(has_right))
    def _():
        graw[2] = graw[1]

    def back_left(c):
        return remote(
            p_left.at[pl.ds(c * step, step), :],
            out_ref.at[pl.ds(2 * width + c * step, step), :],
            (p_send, p_recv), c, me - 1,
        )

    def back_right(c):
        return remote(
            p_right.at[pl.ds(c * step, step), :],
            out_ref.at[pl.ds(c * step, step), :],
            (p_send, p_recv), pieces + c, me + 1,
        )

    both = genes(jnp.concatenate([graw[0], graw[2]], axis=1))
    for c in range(pieces):
        product = jnp.dot(vt[c * step : (c + 1) * step, :], both, preferred_element_type=F32)
        product = (product * scale).astype(BF16)
        p_left[c * step : (c + 1) * step, :] = product[:, 0:BS]
        p_right[c * step : (c + 1) * step, :] = product[:, BS : 2 * BS]

        @pl.when(has_left)
        def _():
            back_left(c).start()

        @pl.when(has_right)
        def _():
            back_right(c).start()

    keep.wait()

    @pl.loop(1, n)
    def _(s):
        exchange(s).wait_send()

    @pl.when(has_left)
    def _():
        genes_left.wait_send()
        for c in range(pieces):
            back_left(c).wait_send()
            back_right(c).wait_recv()

    @pl.when(has_right)
    def _():
        genes_right.wait_send()
        for c in range(pieces):
            back_right(c).wait_send()
            back_left(c).wait_recv()


def on_device(expression, dosages, covariates, window_blocks, window_counts):
    n = lax.axis_size("blk")
    samples, width = dosages.shape
    panels = width // BS
    k = covariates.shape[0]
    slots = window_blocks.shape[1]
    scale = math.sqrt(samples - k) / samples
    any_space = pl.BlockSpec(memory_space=pl.ANY)
    blocks = 3 * panels + slots
    products = pl.pallas_call(
        functools.partial(kernel, n, scale, ROWS),
        out_shape=jax.ShapeDtypeStruct((blocks * BS, BS), BF16),
        in_specs=[any_space] * 3,
        out_specs=any_space,
        scratch_shapes=[
            pltpu.VMEM((k, samples), F32),
            pltpu.VMEM((samples, width), BF16),
            pltpu.VMEM((width, samples), BF16),
            pltpu.VMEM((3, samples, BS), BF16),
            pltpu.VMEM((width, BS), BF16),
            pltpu.VMEM((width, BS), BF16),
            pltpu.VMEM((width, BS), BF16),
            pltpu.VMEM((6 * k, samples), BF16),
            pltpu.VMEM((6 * k, samples), BF16),
            pltpu.VMEM((samples, 6 * k), BF16),
            pltpu.SemaphoreType.DMA((4,)),
            pltpu.SemaphoreType.DMA((n,)),
            pltpu.SemaphoreType.DMA((n,)),
            pltpu.SemaphoreType.DMA((2,)),
            pltpu.SemaphoreType.DMA((2,)),
            pltpu.SemaphoreType.DMA((8,)),
            pltpu.SemaphoreType.DMA((8,)),
        ],
        compiler_params=pltpu.CompilerParams(
            collective_id=0, has_side_effects=True, vmem_limit_bytes=VMEM_BYTES
        ),
    )(expression, dosages, covariates)
    first = window_blocks[0, 0] - (lax.axis_index("blk") - 1) * panels
    listed = lax.dynamic_slice_in_dim(products.reshape(blocks, BS, BS), first, slots, axis=0)
    live = jnp.arange(slots)[None, :] < window_counts[:, None]
    return jnp.where(live[:, :, None, None], listed[None].astype(F32), 0.0)


def solution(mesh):
    in_specs = (
        P("blk", "slab"),
        P(None, ("slab", "blk")),
        P(),
        P(("slab", "blk"), None),
        P(("slab", "blk")),
    )
    out_specs = P(("slab", "blk"), None, None, None)
    return jax.shard_map(
        on_device, mesh=mesh, in_specs=in_specs, out_specs=out_specs, check_vma=False
    )
```

```python
import functools
import math

import jax
import jax.numpy as jnp
from jax import lax
from jax.experimental import pallas as pl
from jax.experimental.pallas import tpu as pltpu
from jax.sharding import PartitionSpec as P

BS = 128
PANEL = 4
ROWS = 256
VMEM_BYTES = 63 * 10**6
MESH = pl.DeviceIdType.MESH
F32 = jnp.float32
BF16 = jnp.bfloat16
NT = (((1,), (1,)), ((), ()))


def split3(x):
    high = x.astype(BF16)
    rest = x - high.astype(F32)
    middle = rest.astype(BF16)
    low = (rest - middle.astype(F32)).astype(BF16)
    return high, middle, low


def whitened(cov):
    k = cov.shape[0]
    zeros = jnp.zeros_like(cov)
    gram = lax.dot_general(
        cov,
        jnp.concatenate([cov, zeros], axis=0),
        NT,
        precision=lax.Precision.HIGHEST,
        preferred_element_type=F32,
    )
    lane = lax.broadcasted_iota(jnp.int32, (8, 2 * k), 1)
    sub = lax.broadcasted_iota(jnp.int32, (8, 2 * k), 0)
    tiles = []
    for t in range(k // 8):
        unit = (lane - k == sub + 8 * t).astype(F32)
        tiles.append(jnp.where(lane < k, gram[8 * t : 8 * t + 8, :], unit))
    for first in range(0, k, PANEL):
        home = first // 8
        live = range(home, k // 8)
        columns = [
            {t: jnp.broadcast_to(tiles[t][:, first + j : first + j + 1], (8, 2 * k)) for t in live}
            for j in range(PANEL)
        ]
        rows = [tiles[home][first % 8 + j : first % 8 + j + 1, :] for j in range(PANEL)]
        for j in range(PANEL):
            at = first % 8 + j
            inverse = 1.0 / columns[j][home][at : at + 1, :]
            factors = {t: columns[j][t] * inverse for t in live}
            factors[home] = jnp.where(sub > at, factors[home], 0.0)
            for later in range(j + 1, PANEL):
                cross = columns[later][home][at : at + 1, :]
                for t in live:
                    columns[later][t] = columns[later][t] - factors[t] * cross
                where = first % 8 + later
                rows[later] = rows[later] - factors[home][where : where + 1, :] * rows[j]
            for t in live:
                tiles[t] = tiles[t] - factors[t] * rows[j]
    scaled = []
    for t in range(k // 8):
        diagonal = jnp.sum(jnp.where(lane == sub + 8 * t, tiles[t], 0.0), axis=1, keepdims=True)
        scaled.append(jnp.where(lane < k, 0.0, tiles[t]) * lax.rsqrt(diagonal))
    inverse_factor = jnp.concatenate(scaled, axis=0)
    return jnp.dot(
        inverse_factor,
        jnp.concatenate([zeros, cov], axis=0),
        precision=lax.Precision.HIGHEST,
        preferred_element_type=F32,
    )


def kernel(
    n, scale, rows,
    expr_ref, dos_ref, cov_ref,
    out_ref,
    cov_v, dos_v, vt, pair, ready, chip_ready, p_own, p_cross, p_chip, q6, qd, qt6,
    local_sem, a2a_send, a2a_recv, edge_send, edge_recv, g_send, g_recv, p_send, p_recv,
):
    me = lax.axis_index("blk")
    samples, width = dos_v.shape
    part = expr_ref.shape[0]
    k = cov_v.shape[0]
    odd = lax.rem(me, 2)
    side = lax.rem(me // 2, 2)
    cross = me - 1 + 2 * odd
    chip = me + 1 - 2 * odd
    at_edge = jnp.logical_or(me == 0, me == n - 1)
    inside = jnp.logical_not(at_edge)
    own_half = 1 - odd
    fellows = n // 2
    rank = (me // 4) * 2 + odd

    barrier = pltpu.get_barrier_semaphore()

    @pl.loop(1, n)
    def _(s):
        pl.semaphore_signal(
            barrier, inc=1, device_id={"blk": lax.rem(me + s, n)}, device_id_type=MESH
        )

    cov_copy = pltpu.make_async_copy(cov_ref, cov_v, local_sem.at[0])
    cov_copy.start()
    dos_copy = pltpu.make_async_copy(dos_ref, dos_v, local_sem.at[1])
    dos_copy.start()
    my_rows = pl.ds(pl.multiple_of(me * part, 16), part)

    def columns(j, count):
        return expr_ref.at[:, pl.ds(pl.multiple_of(j * BS, BS), count * BS)]

    def half(j):
        return pl.ds(pl.multiple_of(j * BS, BS), BS)

    own_pair = pltpu.make_async_copy(
        columns(me - own_half, 2), pair.at[my_rows, :], local_sem.at[2]
    )
    own_single = pltpu.make_async_copy(
        columns(me, 1), pair.at[my_rows, half(own_half)], local_sem.at[2]
    )

    @pl.when(inside)
    def _():
        own_pair.start()

    @pl.when(at_edge)
    def _():
        own_single.start()
        ready[odd] = jnp.zeros((samples, BS), BF16)

    def remote(src, dst, sems, slot, peer):
        return pltpu.make_async_remote_copy(
            src_ref=src,
            dst_ref=dst,
            send_sem=sems[0].at[slot],
            recv_sem=sems[1].at[slot],
            device_id={"blk": peer},
            device_id_type=MESH,
        )

    def peer_of(s):
        index = lax.rem(rank + s, fellows)
        return (index // 2) * 4 + 2 * side + lax.rem(index, 2)

    def shard_pair(s):
        peer = peer_of(s)
        low = jnp.clip(peer - 1 + lax.rem(peer, 2), 0, n - 2)
        return remote(columns(low, 2), pair.at[my_rows, :], (a2a_send, a2a_recv), s, peer)

    def shard_single(s):
        peer = peer_of(s)
        target = pair.at[my_rows, half(1 - lax.rem(peer, 2))]
        return remote(columns(peer, 1), target, (a2a_send, a2a_recv), s, peer)

    def peer_at_edge(s):
        peer = peer_of(s)
        return jnp.logical_or(peer == 0, peer == n - 1)

    far_edge = (1 - side) * (n - 1)
    to_edge = remote(
        columns(far_edge, 1),
        pair.at[my_rows, half(side)],
        (edge_send, edge_recv), rank, far_edge,
    )

    pl.semaphore_wait(barrier, n - 1)

    @pl.loop(1, fellows, unroll=True)
    def _(s):
        @pl.when(peer_at_edge(s))
        def _():
            shard_single(s).start()

        @pl.when(jnp.logical_not(peer_at_edge(s)))
        def _():
            shard_pair(s).start()

    to_edge.start()

    cov_copy.wait()
    q = whitened(cov_v[...])
    qh, qm, ql = split3(q)
    q6[...] = jnp.concatenate([qh, qm, qh, qm, qh, ql], axis=0)
    qd[...] = jnp.concatenate([qh, qm, ql, ql], axis=0)
    first = q6[0 : 2 * k, :].T
    qt6[:, 0 : 2 * k] = first
    qt6[:, 2 * k : 4 * k] = first
    qt6[:, 4 * k : 6 * k] = q6[4 * k : 6 * k, :].T

    dos_copy.wait()

    def variants(at):
        v = dos_v[:, pl.ds(at, rows)].T
        w3 = lax.dot_general(v, qd[...], NT, preferred_element_type=F32)
        w = w3[:, 0 : 2 * k]
        w = w + pltpu.roll(w, k, 1) + w3[:, 2 * k : 4 * k]
        wh, wm, wl = split3(w)
        lane = lax.broadcasted_iota(jnp.int32, w.shape, 1)
        last = jnp.where(lane < k, wl.astype(F32), wh.astype(F32)).astype(BF16)
        w6 = jnp.concatenate([wh, wm, last], axis=1)
        res = v.astype(F32) - jnp.dot(w6, q6[...], preferred_element_type=F32)
        mean = jnp.sum(res * res, axis=1, keepdims=True) * (1.0 / samples)
        vt[pl.ds(at, rows), :] = (res * lax.rsqrt(mean + 1e-06)).astype(BF16)

    chips = n // 4

    def stretch(i, which):
        chunk = lax.rem(me // 4 + i, chips)
        rows_at = pl.ds(pl.multiple_of((chunk * 4 + 2 * which) * part, 16), 2 * part)
        return remote(
            pair.at[rows_at, :], pair.at[rows_at, :], (g_send, g_recv), chunk, cross
        )

    def pass_on(i):
        chunk = lax.rem(me // 4 + i, chips)
        for member in range(2):
            s = lax.rem(rank - chunk * 2 - member + fellows, fellows)

            @pl.when(jnp.logical_and(s > 0, at_edge))
            def _():
                shard_single(s).wait_recv()

            @pl.when(jnp.logical_and(s > 0, inside))
            def _():
                shard_pair(s).wait_recv()

        @pl.when(inside)
        def _():
            stretch(i, side).start()

    @pl.when(inside)
    def _():
        own_pair.wait()

    @pl.when(at_edge)
    def _():
        own_single.wait()

    quarter = width // 4
    for c in range(4):

        @pl.loop(2 * c * chips // 4 if c < 2 else chips, min(2 * c + 2, 4) * chips // 4)
        def _(i):
            pass_on(i)

        @pl.loop(c * quarter // rows, (c + 1) * quarter // rows)
        def _(t):
            variants(pl.multiple_of(t * rows, rows))

    def genes(raw):
        w3 = jnp.dot(
            jnp.concatenate([q6[0 : 2 * k, :], q6[5 * k : 6 * k, :]], axis=0),
            raw,
            preferred_element_type=F32,
        )
        wh, wm, wl = split3(w3[0:k, :] + w3[k : 2 * k, :] + w3[2 * k : 3 * k, :])
        w6 = jnp.concatenate([wh, wh, wm, wm, wl, wh], axis=0)
        res = raw.astype(F32) - jnp.dot(qt6[...], w6, preferred_element_type=F32)
        mean = jnp.sum(res * res, axis=0, keepdims=True) * (1.0 / samples)
        return (res * lax.rsqrt(mean + 1e-06)).astype(BF16)

    @pl.when(inside)
    def _():
        @pl.loop(0, chips)
        def _(i):
            stretch(i, 1 - side).wait_recv()

        both = genes(pair[...])
        ready[0] = both[:, 0:BS]
        ready[1] = both[:, BS : 2 * BS]

    @pl.when(at_edge)
    def _():
        @pl.loop(0, fellows)
        def _(i):
            remote(
                columns(far_edge, 1),
                pair.at[my_rows, half(side)],
                (edge_send, edge_recv), i, far_edge,
            ).wait_recv()

        ready[own_half] = genes(pair[:, half(own_half)])

    share = remote(ready.at[own_half], chip_ready, (g_send, g_recv), chips, chip)
    share.start()

    pieces = 4
    step = width // pieces

    def back_cross(c):
        rows_at = pl.multiple_of(own_half * 2 * width + c * step, BS)
        return remote(
            p_cross.at[pl.ds(c * step, step), :],
            out_ref.at[pl.ds(rows_at, step), :],
            (p_send, p_recv), c, cross,
        )

    back_chip = remote(
        p_chip,
        out_ref.at[pl.ds(pl.multiple_of(odd * 2 * width, BS), width), :],
        (p_send, p_recv), pieces, chip,
    )

    for c in range(pieces):
        product = jnp.dot(
            vt[c * step : (c + 1) * step, :], ready[odd], preferred_element_type=F32
        )
        p_cross[c * step : (c + 1) * step, :] = (product * scale).astype(BF16)

        @pl.when(inside)
        def _():
            back_cross(c).start()

    share.wait_recv()
    local = jnp.concatenate([ready[own_half], chip_ready[...]], axis=1)
    for c in range(pieces):
        product = jnp.dot(vt[c * step : (c + 1) * step, :], local, preferred_element_type=F32)
        product = (product * scale).astype(BF16)
        p_own[c * step : (c + 1) * step, :] = product[:, 0:BS]
        p_chip[c * step : (c + 1) * step, :] = product[:, BS : 2 * BS]
    back_chip.start()
    keep = pltpu.make_async_copy(p_own, out_ref.at[pl.ds(width, width), :], local_sem.at[3])
    keep.start()
    keep.wait()

    @pl.loop(1, fellows, unroll=True)
    def _(s):
        @pl.when(peer_at_edge(s))
        def _():
            shard_single(s).wait_send()

        @pl.when(jnp.logical_not(peer_at_edge(s)))
        def _():
            shard_pair(s).wait_send()

    to_edge.wait_send()
    share.wait_send()
    back_chip.wait()

    @pl.when(inside)
    def _():
        @pl.loop(0, chips)
        def _(i):
            stretch(i, side).wait_send()

        for c in range(pieces):
            back_cross(c).wait()


def on_device(expression, dosages, covariates, window_blocks, window_counts):
    n = lax.axis_size("blk")
    samples, width = dosages.shape
    panels = width // BS
    k = covariates.shape[0]
    slots = window_blocks.shape[1]
    scale = math.sqrt(samples - k) / samples
    any_space = pl.BlockSpec(memory_space=pl.ANY)
    blocks = 3 * panels + slots
    products = pl.pallas_call(
        functools.partial(kernel, n, scale, ROWS),
        out_shape=jax.ShapeDtypeStruct((blocks * BS, BS), BF16),
        in_specs=[any_space] * 3,
        out_specs=any_space,
        scratch_shapes=[
            pltpu.VMEM((k, samples), F32),
            pltpu.VMEM((samples, width), BF16),
            pltpu.VMEM((width, samples), BF16),
            pltpu.VMEM((samples, 2 * BS), BF16),
            pltpu.VMEM((2, samples, BS), BF16),
            pltpu.VMEM((samples, BS), BF16),
            pltpu.VMEM((width, BS), BF16),
            pltpu.VMEM((width, BS), BF16),
            pltpu.VMEM((width, BS), BF16),
            pltpu.VMEM((6 * k, samples), BF16),
            pltpu.VMEM((4 * k, samples), BF16),
            pltpu.VMEM((samples, 6 * k), BF16),
            pltpu.SemaphoreType.DMA((4,)),
            pltpu.SemaphoreType.DMA((n // 2,)),
            pltpu.SemaphoreType.DMA((n // 2,)),
            pltpu.SemaphoreType.DMA((n // 2,)),
            pltpu.SemaphoreType.DMA((n // 2,)),
            pltpu.SemaphoreType.DMA((n // 4 + 1,)),
            pltpu.SemaphoreType.DMA((n // 4 + 1,)),
            pltpu.SemaphoreType.DMA((5,)),
            pltpu.SemaphoreType.DMA((5,)),
        ],
        compiler_params=pltpu.CompilerParams(
            collective_id=0, has_side_effects=True, vmem_limit_bytes=VMEM_BYTES
        ),
    )(expression, dosages, covariates)
    first = window_blocks[0, 0] - (lax.axis_index("blk") - 1) * panels
    listed = lax.dynamic_slice_in_dim(products.reshape(blocks, BS, BS), first, slots, axis=0)
    live = jnp.arange(slots)[None, :] < window_counts[:, None]
    return jnp.where(live[:, :, None, None], listed[None].astype(F32), 0.0)


def solution(mesh):
    in_specs = (
        P("blk", "slab"),
        P(None, ("slab", "blk")),
        P(),
        P(("slab", "blk"), None),
        P(("slab", "blk")),
    )
    out_specs = P(("slab", "blk"), None, None, None)
    return jax.shard_map(
        on_device, mesh=mesh, in_specs=in_specs, out_specs=out_specs, check_vma=False
    )
```
